32 devices in a mesh: rows: 8 (over z, core), cols: 4 (over y, x).
Axes of the slice: x: 2, y: 2, z: 4, core: 2. Of those that a mesh axis runs over, the one named last changes fastest.
Arguments:
- tensor: float32 [32, 1024, 512], P(None, 'rows', 'cols'), may hold values from -307200 to 307200
- second_init: float32 [512, 64], P('cols'), may hold values from -6 to 6
- third_init: float32 [32, 64], replicated, may hold values from -6 to 6
Outputs:
- first: float32 [1024, 64], P('rows')
- second: float32 [512, 64], P('cols')
- third: float32 [32, 64], replicated
The draws below stay inside these ranges and needn't reach their ends.
All inputs are finite; a program needn't handle non-finite values.
Results may differ from the reference program's by a relative error of at most 0.0003.
Values sent between devices are 32-bit elements; how exact they have to be, the bound alone decides.
A program may use at most 64 MiB of HBM per device.

```python
import jax
import jax.numpy as jnp
from jax import lax

K = 32
R = 64
ITERS = 5
I = 1024
J = 512


def draw_tensor(key, part):
    key_noise = jax.random.fold_in(key, 11)
    key_rows = jax.random.fold_in(key, 12)
    key_cols = jax.random.fold_in(key, 13)
    key_time = jax.random.fold_in(key, 14)
    noise = jnp.clip(jax.random.normal(key_noise, (K, I, J), jnp.float32), -6.0, 6.0)
    spread = 10.0
    row_place = jnp.arange(I, dtype=jnp.float32) / I
    col_place = jnp.arange(J, dtype=jnp.float32) / J
    row_scale = jnp.power(3.0, row_place) * jnp.power(spread, jax.random.uniform(key_rows, (I,), jnp.float32))
    col_scale = jnp.power(3.0, col_place) * jnp.power(spread, jax.random.uniform(key_cols, (J,), jnp.float32))
    time_scale = jnp.power(2.0, jax.random.uniform(key_time, (K,), jnp.float32, -1.0, 1.0))
    overall = float((I * J) ** 0.5) / 30.0
    values = noise * time_scale[:, None, None] * row_scale[None, :, None] * col_scale[None, None, :]
    return (values * overall).astype(jnp.float32)


def block_levels(rng, extent, cuts, least, high):
    factor_of = 1.0
    for position, shards_of in cuts:
        steps = jax.random.uniform(jax.random.fold_in(jax.random.fold_in(rng, 6), position), (shards_of,), jnp.float32, least / len(cuts), high / len(cuts))
        factor_of = factor_of * jnp.repeat(jnp.exp(steps), extent[position] // shards_of).reshape((-1,) + (1,) * (len(extent) - 1 - position))
    return factor_of


def normal_values(own_key, shape, scale, reach, shards=(), kind=jnp.bfloat16):
    loudness = block_levels(own_key, shape, shards, -0.22, 0.18) if shards else 1.0
    entries = jax.random.normal(own_key, shape, jnp.float32) * scale * loudness
    return jnp.minimum(jnp.maximum(entries, -reach), reach).astype(kind)


def setup_inputs(seed: int = 0) -> dict:
    seeds = jax.random.split(jax.random.key(seed), 4)
    return {
        "tensor": draw_tensor(jax.random.fold_in(seeds[3], 71), 0),
        "second_init": normal_values(seeds[1], (J, R), 1.0, 6.0, ((0, 4),), jnp.float32),
        "third_init": normal_values(seeds[2], (K, R), 1.0, 6.0, (), jnp.float32),
    }


EPSILON = 1e-05
HIGHEST = lax.Precision.HIGHEST

def solve_right(rhs_rows, system):
    cholesky_low = jnp.linalg.cholesky(system)
    halfway = lax.linalg.triangular_solve(cholesky_low, rhs_rows, left_side=False, lower=True, transpose_a=True)
    return lax.linalg.triangular_solve(cholesky_low, halfway, left_side=False, lower=True)

def unit_scale(factor):
    squares = lax.optimization_barrier(jnp.sum(factor * factor, axis=0)) / factor.shape[0]
    return factor / jnp.sqrt(squares + EPSILON)

def gram_local(factor):
    return jnp.dot(factor.T.astype(jnp.float32), factor.astype(jnp.float32), precision=HIGHEST, preferred_element_type=jnp.float32)

def reference(tensor, second_init, third_init):
    second = unit_scale(second_init)
    third = third_init
    gram_second = gram_local(second)
    gram_third = gram_local(third)
    first = None
    for sweep_index in range(ITERS):
        contract_first = lax.dot_general(second.astype(jnp.float32), tensor.astype(jnp.float32), (((0,), (2,)), ((), ())), precision=HIGHEST, preferred_element_type=jnp.float32)
        mttkrp_first = jnp.einsum('rki,kr->ir', contract_first, third, precision=HIGHEST)
        first = unit_scale(solve_right(mttkrp_first, gram_third * gram_second))
        gram_first = gram_local(first)
        contract_second = lax.dot_general(first.astype(jnp.float32), tensor.astype(jnp.float32), (((0,), (1,)), ((), ())), precision=HIGHEST, preferred_element_type=jnp.float32)
        mttkrp_second = jnp.einsum('rkj,kr->jr', contract_second, third, precision=HIGHEST)
        second = unit_scale(solve_right(mttkrp_second, gram_third * gram_first))
        gram_second = gram_local(second)
        mttkrp_third = jnp.einsum('rkj,jr->kr', contract_second, second, precision=HIGHEST)
        third = solve_right(mttkrp_third, gram_first * gram_second)
        gram_third = gram_local(third)
    return (first, second, third)
```

```python
import functools

import jax
import jax.numpy as jnp
from jax import lax
from jax.experimental import pallas as pl
from jax.experimental.pallas import tpu as pltpu
from jax.sharding import PartitionSpec as P

ITERS = 5
EPSILON = 1e-05
HIGHEST = lax.Precision.HIGHEST
MESH = pl.DeviceIdType.MESH
PANEL = 8


def dot_f32(a, b):
    return jnp.dot(a, b, precision=HIGHEST, preferred_element_type=jnp.float32)


def lane_of(shape):
    return lax.broadcasted_iota(jnp.int32, shape, len(shape) - 1)


def swap_halves(x):
    return pltpu.roll(x, x.shape[1] // 2, axis=1)


def pack(x):
    n = x.shape[0] // 2
    return jnp.where(lane_of((n, x.shape[1])) < x.shape[1] // 2, x[:n], x[n:])


def unpack(x):
    other = swap_halves(x)
    left = lane_of(x.shape) < x.shape[1] // 2
    return jnp.concatenate([jnp.where(left, x, other), jnp.where(left, other, x)], axis=0)


def gram_doubled(x, rank):
    return dot_f32(x.T, x)[:rank]


def gram_scale(raw_gram, total):
    rank, wide = raw_gram.shape
    rows = lax.broadcasted_iota(jnp.int32, (rank, wide), 0)
    lanes = lane_of((rank, wide))
    diag = jnp.where((lanes == rows) | (lanes == rows + rank), raw_gram, 0.0)
    inv_row = 1.0 / jnp.sqrt(jnp.sum(diag, axis=0, keepdims=True) / total + EPSILON)
    squares_col = 0.5 * jnp.sum(diag, axis=1, keepdims=True)
    inv_col = 1.0 / jnp.sqrt(squares_col / total + EPSILON)
    return raw_gram * inv_col * inv_row, inv_row


def inverse_blocks(count, a):
    rank, wide = a.shape
    lane = lane_of((1, wide)) % rank
    sub = lax.broadcasted_iota(jnp.int32, (PANEL, wide), 0)

    def block(_, a):
        cols = [jnp.broadcast_to(a[:, q : q + 1], (rank, wide)) for q in range(PANEL)]
        for p in range(PANEL):
            here = cols[p]
            inv = 1.0 / here[p : p + 1]
            row = jnp.where(lane == p, -inv, a[p : p + 1] * inv)
            new = jnp.where(lane == p, 0.0, a) - here * row
            a = jnp.concatenate([jnp.where(sub == p, row, new[:PANEL]), new[PANEL:]], axis=0)
            for q in range(p + 1, PANEL):
                share = cols[q][p : p + 1] * inv
                new = cols[q] - here * share
                cols[q] = jnp.concatenate(
                    [jnp.where(sub == p, share, new[:PANEL]), new[PANEL:]], axis=0
                )
        a = pltpu.roll(a, wide - PANEL, axis=1)
        return jnp.concatenate([a[PANEL:], a[:PANEL]], axis=0)

    return lax.fori_loop(0, count, block, a)


def inverse(system):
    return -inverse_blocks(system.shape[0] // PANEL, system)


def solve_packed(packed, inv):
    zero = jnp.zeros_like(inv)
    top = dot_f32(packed, jnp.concatenate([inv, zero], axis=0))
    low = dot_f32(packed, jnp.concatenate([zero, inv], axis=0))
    return jnp.concatenate([top, low], axis=0)


def split_weights(x):
    high = x.astype(jnp.bfloat16).astype(jnp.float32)
    mixed = jnp.where(lane_of(x.shape) < x.shape[1] // 2, high, x - high).astype(jnp.bfloat16)
    return jnp.concatenate([mixed, mixed], axis=0)


def kernel(
    nr,
    nc,
    tensor,
    second_in,
    third_in,
    first_out,
    second_out,
    third_out,
    by_row,
    by_col,
    contracted,
    weights,
    first_d,
    second_d,
    third_d,
    gram1,
    gram2,
    gram3,
    m3_rows,
    m1_buf,
    g1_src,
    g1_buf,
    g1_all,
    m2_src,
    m2_buf,
    m2_all,
    g2_buf,
    m3_buf,
    m3_all,
    col_send,
    col_recv,
    row_send,
    row_recv,
):
    K, I, J = tensor.shape
    R = second_in.shape[1]
    my_row = lax.axis_index("rows")
    my_col = lax.axis_index("cols")

    def col_peer(d):
        return lax.rem(my_col + d, nc)

    def row_peer(d):
        return lax.rem(my_row + d, nr)

    def col_copies(kind, buf):
        return [
            pltpu.make_async_remote_copy(
                src_ref=buf.at[my_col],
                dst_ref=buf.at[my_col],
                send_sem=col_send.at[kind, d - 1],
                recv_sem=col_recv.at[kind, d - 1],
                device_id=(my_row, col_peer(d)),
                device_id_type=MESH,
            )
            for d in range(1, nc)
        ]

    def row_copies(kind, src, dst, scatter=False):
        return [
            pltpu.make_async_remote_copy(
                src_ref=src.at[row_peer(d)] if scatter else src.at[my_row],
                dst_ref=dst.at[my_row],
                send_sem=row_send.at[kind, d - 1],
                recv_sem=row_recv.at[kind, d - 1],
                device_id=(row_peer(d), my_col),
                device_id_type=MESH,
            )
            for d in range(1, nr)
        ]

    def start(copies):
        for copy in copies:
            copy.start()
        return copies

    def wait(copies):
        for copy in copies:
            copy.wait()

    def total(buf, n):
        out = buf[0]
        for s in range(1, n):
            out = out + buf[s]
        return out

    def joined(buf, n):
        return jnp.concatenate([buf[s] for s in range(n)], axis=0)

    barrier = pltpu.get_barrier_semaphore()
    for d in range(1, nc):
        pl.semaphore_signal(barrier, inc=1, device_id=(my_row, col_peer(d)), device_id_type=MESH)
    for d in range(1, nr):
        pl.semaphore_signal(barrier, inc=1, device_id=(row_peer(d), my_col), device_id_type=MESH)

    start_second = second_in[...]
    start_second = jnp.concatenate([start_second, start_second], axis=1)
    start_third = third_in[...]
    start_third = jnp.concatenate([start_third, start_third], axis=1)
    third_d[...] = start_third
    g2_buf[my_col] = pack(gram_doubled(start_second, R))
    pl.semaphore_wait(barrier, nc - 1 + nr - 1)
    copies = start(col_copies(1, g2_buf))
    gram3[...] = gram_doubled(start_third, R)

    def split_slice(k, _):
        rows = pl.ds(pl.multiple_of(k * I, I), I)
        block = tensor[k]
        high = block.astype(jnp.bfloat16)
        by_row[rows, :J] = high
        by_row[rows, J:] = (block - high.astype(jnp.float32)).astype(jnp.bfloat16)
        turned = block.T
        rows = pl.ds(pl.multiple_of(k * J, J), J)
        high = turned.astype(jnp.bfloat16)
        by_col[rows, :I] = high
        by_col[rows, I:] = (turned - high.astype(jnp.float32)).astype(jnp.bfloat16)
        return 0

    lax.fori_loop(0, K, split_slice, 0)
    wait(copies)
    gram, inv_scale = gram_scale(unpack(total(g2_buf, nc)), J * nc)
    gram2[...] = gram
    second_d[...] = start_second * inv_scale

    UNROLL = 8

    def contract(source, extent, keep):
        def step(o, acc):
            for u in range(UNROLL):
                k = o * UNROLL + u
                rows = pl.ds(pl.multiple_of(k * extent, extent), extent)
                part = jnp.dot(source[rows, :], weights[...], preferred_element_type=jnp.float32)
                if keep:
                    contracted[k] = part
                acc = acc + part * third_d[pl.ds(k, 1), :]
            return acc

        acc = lax.fori_loop(0, K // UNROLL, step, jnp.zeros((extent, 2 * R), jnp.float32))
        return acc + swap_halves(acc)

    def sweep(_, carry):
        weights[...] = split_weights(second_d[...])
        m1_buf[my_col] = pack(contract(by_row, I, False))
        m1_copies = start(col_copies(0, m1_buf))
        inv = inverse(gram3[...] * gram2[...])
        wait(m1_copies)
        raw1 = solve_packed(total(m1_buf, nc), inv)

        packed = pack(gram_doubled(raw1, R))
        share = packed.shape[0] // nc
        for c in range(nc):
            g1_src[c] = packed[c * share : (c + 1) * share]
        g1_buf[my_row] = g1_src[my_col]
        g1_copies = start(row_copies(0, g1_buf, g1_buf))
        weights[...] = split_weights(raw1)
        packed = pack(contract(by_col, J, True))
        share = packed.shape[0] // nr
        for r in range(nr):
            m2_src[r] = packed[r * share : (r + 1) * share]
        m2_buf[my_row] = m2_src[my_row]
        m2_copies = start(row_copies(1, m2_src, m2_buf, scatter=True))
        wait(g1_copies)
        g1_all[my_col] = total(g1_buf, nr)
        g1_copies = start(col_copies(2, g1_all))
        wait(m2_copies)
        m2_all[my_row] = total(m2_buf, nr)
        m2_copies = start(row_copies(2, m2_all, m2_all))
        wait(g1_copies)
        gram, scale1 = gram_scale(unpack(joined(g1_all, nc)), I * nr)
        gram1[...] = gram
        first_d[...] = raw1 * scale1

        inv = inverse(gram3[...] * gram)
        wait(m2_copies)
        raw2 = solve_packed(joined(m2_all, nr) * scale1, inv)
        g2_buf[my_col] = pack(gram_doubled(raw2, R))
        g2_copies = start(col_copies(1, g2_buf))

        scaled = raw2 * scale1
        for k in range(K):
            m3_rows[k : k + 1] = jnp.sum(contracted[k] * scaled, axis=0, keepdims=True)
        m3 = m3_rows[...]
        m3_buf[my_row] = pack(m3 + swap_halves(m3))
        m3_copies = start(row_copies(3, m3_buf, m3_buf))
        wait(g2_copies)
        gram, scale2 = gram_scale(unpack(total(g2_buf, nc)), J * nc)
        gram2[...] = gram
        second_d[...] = raw2 * scale2
        wait(m3_copies)
        m3_all[my_col] = total(m3_buf, nr)
        m3_copies = start(col_copies(3, m3_all))
        inv = inverse(gram1[...] * gram)
        wait(m3_copies)
        third = solve_packed(total(m3_all, nc) * scale2, inv)
        third_d[...] = third
        gram3[...] = gram_doubled(third, R)
        return carry

    lax.fori_loop(0, ITERS, sweep, 0)
    first_out[...] = first_d[:, :R]
    second_out[...] = second_d[:, :R]
    third_out[...] = third_d[:, :R]


def per_device(nr, nc, tensor, second_init, third_init):
    K, I, J = tensor.shape
    R = second_init.shape[1]
    wide = 2 * R
    f32 = jnp.float32
    half = R // 2

    def vmem(*shape):
        return pltpu.VMEM(shape, f32)

    return pl.pallas_call(
        functools.partial(kernel, nr, nc),
        out_shape=(
            jax.ShapeDtypeStruct((I, R), f32),
            jax.ShapeDtypeStruct((J, R), f32),
            jax.ShapeDtypeStruct((K, R), f32),
        ),
        in_specs=[pl.BlockSpec(memory_space=pltpu.VMEM)] * 3,
        out_specs=(pl.BlockSpec(memory_space=pltpu.VMEM),) * 3,
        scratch_shapes=[
            pltpu.VMEM((K * I, 2 * J), jnp.bfloat16),
            pltpu.VMEM((K * J, 2 * I), jnp.bfloat16),
            vmem(K, J, wide),
            pltpu.VMEM((2 * J, wide), jnp.bfloat16),
            vmem(I, wide),
            vmem(J, wide),
            vmem(K, wide),
            vmem(R, wide),
            vmem(R, wide),
            vmem(R, wide),
            vmem(K, wide),
            vmem(nc, I // 2, wide),
            vmem(nc, half // nc, wide),
            vmem(nr, half // nc, wide),
            vmem(nc, half // nc, wide),
            vmem(nr, J // 2 // nr, wide),
            vmem(nr, J // 2 // nr, wide),
            vmem(nr, J // 2 // nr, wide),
            vmem(nc, half, wide),
            vmem(nr, K // 2, wide),
            vmem(nc, K // 2, wide),
            pltpu.SemaphoreType.DMA((4, nc - 1)),
            pltpu.SemaphoreType.DMA((4, nc - 1)),
            pltpu.SemaphoreType.DMA((4, nr - 1)),
            pltpu.SemaphoreType.DMA((4, nr - 1)),
        ],
        compiler_params=pltpu.CompilerParams(
            collective_id=0, has_side_effects=True, vmem_limit_bytes=32 * 1024 * 1024
        ),
        cost_estimate=pl.CostEstimate(
            flops=ITERS * 2 * 2 * K * I * J * 2 * wide, bytes_accessed=4 * K * I * J, transcendentals=0
        ),
        name="als_sweeps",
    )(tensor, second_init, third_init)


def solution(mesh):
    return jax.shard_map(
        functools.partial(per_device, mesh.shape["rows"], mesh.shape["cols"]),
        mesh=mesh,
        in_specs=(P(None, "rows", "cols"), P("cols", None), P()),
        out_specs=(P("rows", None), P("cols", None), P()),
        check_vma=False,
    )
```

```python
import functools

import jax
import jax.numpy as jnp
from jax import lax
from jax.experimental import pallas as pl
from jax.experimental.pallas import tpu as pltpu
from jax.sharding import PartitionSpec as P

ITERS = 5
EPSILON = 1e-05
HIGHEST = lax.Precision.HIGHEST
MESH = pl.DeviceIdType.MESH
PANEL = 8


def dot_f32(a, b):
    return jnp.dot(a, b, precision=HIGHEST, preferred_element_type=jnp.float32)


def lane_of(shape):
    return lax.broadcasted_iota(jnp.int32, shape, len(shape) - 1)


def swap_halves(x):
    return pltpu.roll(x, x.shape[1] // 2, axis=1)


def pack(x):
    n = x.shape[0] // 2
    return jnp.where(lane_of((n, x.shape[1])) < x.shape[1] // 2, x[:n], x[n:])


def unpack(x):
    other = swap_halves(x)
    left = lane_of(x.shape) < x.shape[1] // 2
    return jnp.concatenate([jnp.where(left, x, other), jnp.where(left, other, x)], axis=0)


def gram_doubled(x, rank):
    return dot_f32(x.T, x)[:rank]


def diag_mask(rank, wide):
    rows = lax.broadcasted_iota(jnp.int32, (rank, wide), 0)
    lanes = lane_of((rank, wide))
    return (lanes == rows) | (lanes == rows + rank)


def col_scale(raw_gram, total):
    diag = jnp.where(diag_mask(*raw_gram.shape), raw_gram, 0.0)
    return jnp.sqrt(jnp.sum(diag, axis=0, keepdims=True) / total + EPSILON)


def balance(system):
    diag = jnp.where(diag_mask(*system.shape), system, 0.0)
    by_lane = lax.rsqrt(jnp.sum(diag, axis=0, keepdims=True))
    by_sub = lax.rsqrt(0.5 * jnp.sum(diag, axis=1, keepdims=True))
    return system * by_sub * by_lane, by_lane, by_sub


def sweep_blocks(a, first, last):
    rank, wide = a.shape
    tiles = rank // PANEL
    tile = (PANEL, wide)
    lane = lane_of(tile) % rank
    sub = lax.broadcasted_iota(jnp.int32, tile, 0)
    a = a.reshape(tiles, PANEL, wide)

    for b in range(first, last):
        base = b * PANEL

        def row(x, p):
            return jnp.broadcast_to(x[b, p : p + 1], tile)

        def put(x, p, top, low):
            mid = jnp.where(sub == p, top, jnp.where(sub == p + 1, low, x[b]))[None]
            parts = [x[:b]] * (b > 0) + [mid] + [x[b + 1 :]] * (b + 1 < tiles)
            return jnp.concatenate(parts, axis=0)

        cols = [
            jnp.broadcast_to(a[:, :, base + q : base + q + 1], a.shape) for q in range(PANEL)
        ]
        for p in range(0, PANEL, 2):
            u, v = cols[p], cols[p + 1]
            uu, uv, vv = row(u, p), row(u, p + 1), row(v, p + 1)
            inv = 1.0 / (uu * vv - uv * uv)
            iu, iv, ic = vv * inv, uu * inv, -(uv * inv)
            for q in range(p + 2, PANEL):
                x, y = row(cols[q], p), row(cols[q], p + 1)
                top, low = iu * x + ic * y, ic * x + iv * y
                cols[q] = put(cols[q] - u * top - v * low, p, top, low)
            x, y = row(a, p), row(a, p + 1)
            top, low = iu * x + ic * y, ic * x + iv * y
            at_u, at_v = lane == base + p, lane == base + p + 1
            top = jnp.where(at_u, -iu, jnp.where(at_v, -ic, top))
            low = jnp.where(at_u, -ic, jnp.where(at_v, -iv, low))
            kept = jnp.where((at_u | at_v)[None], 0.0, a)
            a = put(kept - u * top - v * low, p, top, low)
    return a.reshape(rank, wide)


def solve_packed(packed, minus_inv):
    wide = minus_inv.shape[1]
    inv = -minus_inv
    zero = jnp.zeros_like(inv)
    both = jnp.concatenate(
        [jnp.concatenate([inv, zero], axis=1), jnp.concatenate([zero, inv], axis=1)], axis=0
    )
    out = dot_f32(packed, both)
    return jnp.concatenate([out[:, :wide], out[:, wide:]], axis=0)


def split_weights(x):
    high = x.astype(jnp.bfloat16).astype(jnp.float32)
    mixed = jnp.where(lane_of(x.shape) < x.shape[1] // 2, high, x - high).astype(jnp.bfloat16)
    return jnp.concatenate([mixed, mixed], axis=0)


def kernel(
    nr,
    nc,
    tensor_in,
    second_in,
    third_in,
    first_out,
    second_out,
    third_out,
    tensor,
    by_row,
    by_col,
    contracted,
    weights,
    first_d,
    second_d,
    third_d,
    third_raw,
    third_inv,
    scale2_row,
    gram2,
    gram3,
    m3_rows,
    m1_buf,
    g1_src,
    g1_buf,
    g1_all,
    m2_src,
    m2_buf,
    m2_all,
    g2_buf,
    m3_buf,
    m3_all,
    col_send,
    col_recv,
    row_send,
    row_recv,
    load_sem,
):
    K, I, J = tensor.shape
    R = second_in.shape[0]
    my_row = lax.axis_index("rows")
    my_col = lax.axis_index("cols")

    def col_peer(d):
        return lax.rem(my_col + d, nc)

    def row_peer(d):
        return lax.rem(my_row + d, nr)

    def col_copies(kind, buf):
        return [
            pltpu.make_async_remote_copy(
                src_ref=buf.at[my_col],
                dst_ref=buf.at[my_col],
                send_sem=col_send.at[kind, d - 1],
                recv_sem=col_recv.at[kind, d - 1],
                device_id=(my_row, col_peer(d)),
                device_id_type=MESH,
            )
            for d in range(1, nc)
        ]

    def row_copies(kind, src, dst, scatter=False):
        return [
            pltpu.make_async_remote_copy(
                src_ref=src.at[row_peer(d)] if scatter else src.at[my_row],
                dst_ref=dst.at[my_row],
                send_sem=row_send.at[kind, d - 1],
                recv_sem=row_recv.at[kind, d - 1],
                device_id=(row_peer(d), my_col),
                device_id_type=MESH,
            )
            for d in range(1, nr)
        ]

    def start(copies):
        for copy in copies:
            copy.start()
        return copies

    def wait(copies):
        for copy in copies:
            copy.wait()

    def total(buf, n):
        out = buf[0]
        for s in range(1, n):
            out = out + buf[s]
        return out

    def joined(buf, n):
        return jnp.concatenate([buf[s] for s in range(n)], axis=0)

    barrier = pltpu.get_barrier_semaphore()
    for d in range(1, nc):
        pl.semaphore_signal(barrier, inc=1, device_id=(my_row, col_peer(d)), device_id_type=MESH)
    for d in range(1, nr):
        pl.semaphore_signal(barrier, inc=1, device_id=(row_peer(d), my_col), device_id_type=MESH)

    GROUP = 8
    loads = [
        pltpu.make_async_copy(
            tensor_in.at[pl.ds(g * GROUP, GROUP)], tensor.at[pl.ds(g * GROUP, GROUP)], load_sem.at[g]
        )
        for g in range(K // GROUP)
    ]
    start(loads)
    start_second = second_in[...]
    start_second = jnp.concatenate([start_second, start_second], axis=0).T
    start_third = third_in[...]
    start_third = jnp.concatenate([start_third, start_third], axis=1)
    g2_buf[my_col] = pack(gram_doubled(start_second, R))
    pl.semaphore_wait(barrier, nc - 1 + nr - 1)
    copies = start(col_copies(1, g2_buf))

    def settle_third(third):
        inv_norm = 1.0 / jnp.sqrt(jnp.sum(third * third, axis=0, keepdims=True))
        unit = third * inv_norm
        third_d[...] = unit
        third_inv[...] = inv_norm
        gram3[...] = gram_doubled(unit, R)

    settle_third(start_third)

    def split_slice(k, _):
        rows = pl.ds(pl.multiple_of(k * I, I), I)
        block = tensor[k]
        high = block.astype(jnp.bfloat16)
        by_row[rows, :J] = high
        by_row[rows, J:] = (block - high.astype(jnp.float32)).astype(jnp.bfloat16)
        turned = block.T
        rows = pl.ds(pl.multiple_of(k * J, J), J)
        high = turned.astype(jnp.bfloat16)
        by_col[rows, :I] = high
        by_col[rows, I:] = (turned - high.astype(jnp.float32)).astype(jnp.bfloat16)
        return 0

    for g, load in enumerate(loads):
        load.wait()
        lax.fori_loop(g * GROUP, (g + 1) * GROUP, split_slice, 0)
    wait(copies)
    gram = unpack(total(g2_buf, nc))
    gram2[...] = gram
    scale = col_scale(gram, J * nc)
    scale2_row[...] = scale
    second_d[...] = start_second / scale

    def contract(source, extent, keep):
        def step(o, acc):
            rows = pl.ds(pl.multiple_of(o * GROUP * extent, GROUP * extent), GROUP * extent)
            part = jnp.dot(source[rows, :], weights[...], preferred_element_type=jnp.float32)
            for u in range(GROUP):
                k = o * GROUP + u
                one = part[u * extent : (u + 1) * extent]
                if keep:
                    contracted[k] = one
                acc = acc + one * third_d[pl.ds(k, 1), :]
            return acc

        acc = lax.fori_loop(0, K // GROUP, step, jnp.zeros((extent, 2 * R), jnp.float32))
        return acc + swap_halves(acc)

    BLOCKS = R // PANEL

    def sweep(_, carry):
        weights[...] = split_weights(second_d[...])
        m1_buf[my_col] = pack(contract(by_row, I, False))
        m1_copies = start(col_copies(0, m1_buf))
        system, by_lane, _ = balance(gram3[...] * gram2[...])
        inv = sweep_blocks(system, 0, BLOCKS)
        around = by_lane * scale2_row[...]
        wait(m1_copies)
        raw1 = solve_packed(total(m1_buf, nc) * around, inv) * (around * third_inv[...])

        packed = pack(gram_doubled(raw1, R))
        share = packed.shape[0] // nc
        for c in range(nc):
            g1_src[c] = packed[c * share : (c + 1) * share]
        g1_buf[my_row] = g1_src[my_col]
        g1_copies = start(row_copies(0, g1_buf, g1_buf))
        weights[...] = split_weights(raw1)
        packed = pack(contract(by_col, J, True))
        share = packed.shape[0] // nr
        for r in range(nr):
            m2_src[r] = packed[r * share : (r + 1) * share]
        m2_buf[my_row] = m2_src[my_row]
        m2_copies = start(row_copies(1, m2_src, m2_buf, scatter=True))
        wait(g1_copies)
        g1_all[my_col] = total(g1_buf, nr)
        g1_copies = start(col_copies(2, g1_all))
        wait(m2_copies)
        m2_all[my_row] = total(m2_buf, nr)
        m2_copies = start(row_copies(2, m2_all, m2_all))
        wait(g1_copies)

        gram1 = unpack(joined(g1_all, nc))
        system, by_lane1, by_sub1 = balance(gram3[...] * gram1)
        inv = sweep_blocks(system, 0, BLOCKS)
        gram1 = gram1 * by_sub1 * by_lane1
        scale1 = col_scale(unpack(joined(g1_all, nc)), I * nr)
        first_d[...] = raw1 / scale1
        wait(m2_copies)
        raw2 = solve_packed(joined(m2_all, nr) * by_lane1, inv) * (by_lane1 * scale1)
        g2_buf[my_col] = pack(gram_doubled(raw2, R))
        g2_copies = start(col_copies(1, g2_buf))

        scaled = raw2 / scale1
        for k in range(K):
            m3_rows[k : k + 1] = jnp.sum(contracted[k] * scaled, axis=0, keepdims=True)
        m3 = m3_rows[...]
        m3_buf[my_row] = pack(m3 + swap_halves(m3))
        m3_copies = start(row_copies(3, m3_buf, m3_buf))
        wait(g2_copies)
        gram = unpack(total(g2_buf, nc))
        gram2[...] = gram
        system, by_lane, _ = balance(gram1 * gram)
        inv = sweep_blocks(system, 0, BLOCKS // 2)
        wait(m3_copies)
        m3_all[my_col] = total(m3_buf, nr)
        m3_copies = start(col_copies(3, m3_all))
        inv = sweep_blocks(inv, BLOCKS // 2, BLOCKS)
        scale2 = col_scale(gram, J * nc)
        scale2_row[...] = scale2
        second_d[...] = raw2 / scale2
        around = by_lane * by_lane1 * scale1
        wait(m3_copies)
        third = solve_packed(total(m3_all, nc) * around, inv) * (around * scale2)
        third_raw[...] = third
        settle_third(third)
        return carry

    lax.fori_loop(0, ITERS, sweep, 0)
    first_out[...] = first_d[...].T[:R]
    second_out[...] = second_d[...].T[:R]
    third_out[...] = third_raw[:, :R]


def per_device(nr, nc, tensor, second_init, third_init):
    K, I, J = tensor.shape
    R = second_init.shape[1]
    wide = 2 * R
    f32 = jnp.float32
    half = R // 2

    def vmem(*shape):
        return pltpu.VMEM(shape, f32)

    first, second, third = pl.pallas_call(
        functools.partial(kernel, nr, nc),
        out_shape=(
            jax.ShapeDtypeStruct((R, I), f32),
            jax.ShapeDtypeStruct((R, J), f32),
            jax.ShapeDtypeStruct((K, R), f32),
        ),
        in_specs=[pl.BlockSpec(memory_space=pl.ANY)] + [pl.BlockSpec(memory_space=pltpu.VMEM)] * 2,
        out_specs=(pl.BlockSpec(memory_space=pltpu.VMEM),) * 3,
        scratch_shapes=[
            vmem(K, I, J),
            pltpu.VMEM((K * I, 2 * J), jnp.bfloat16),
            pltpu.VMEM((K * J, 2 * I), jnp.bfloat16),
            vmem(K, J, wide),
            pltpu.VMEM((2 * J, wide), jnp.bfloat16),
            vmem(I, wide),
            vmem(J, wide),
            vmem(K, wide),
            vmem(K, wide),
            vmem(1, wide),
            vmem(1, wide),
            vmem(R, wide),
            vmem(R, wide),
            vmem(K, wide),
            vmem(nc, I // 2, wide),
            vmem(nc, half // nc, wide),
            vmem(nr, half // nc, wide),
            vmem(nc, half // nc, wide),
            vmem(nr, J // 2 // nr, wide),
            vmem(nr, J // 2 // nr, wide),
            vmem(nr, J // 2 // nr, wide),
            vmem(nc, half, wide),
            vmem(nr, K // 2, wide),
            vmem(nc, K // 2, wide),
            pltpu.SemaphoreType.DMA((4, nc - 1)),
            pltpu.SemaphoreType.DMA((4, nc - 1)),
            pltpu.SemaphoreType.DMA((4, nr - 1)),
            pltpu.SemaphoreType.DMA((4, nr - 1)),
            pltpu.SemaphoreType.DMA((K // 8,)),
        ],
        compiler_params=pltpu.CompilerParams(
            collective_id=0, has_side_effects=True, vmem_limit_bytes=56 * 1024 * 1024
        ),
        cost_estimate=pl.CostEstimate(
            flops=ITERS * 2 * 2 * K * I * J * 2 * wide, bytes_accessed=4 * K * I * J, transcendentals=0
        ),
        name="als_sweeps",
    )(tensor, second_init.T, third_init)
    return first.T, second.T, third


def solution(mesh):
    return jax.shard_map(
        functools.partial(per_device, mesh.shape["rows"], mesh.shape["cols"]),
        mesh=mesh,
        in_specs=(P(None, "rows", "cols"), P("cols", None), P()),
        out_specs=(P("rows", None), P("cols", None), P()),
        check_vma=False,
    )
```

```python
import functools

import jax
import jax.numpy as jnp
from jax import lax
from jax.experimental import pallas as pl
from jax.experimental.pallas import tpu as pltpu
from jax.sharding import PartitionSpec as P

ITERS = 5
EPSILON = 1e-05
HIGHEST = lax.Precision.HIGHEST
MESH = pl.DeviceIdType.MESH
PANEL = 8


def dot_f32(a, b):
    return jnp.dot(a, b, precision=HIGHEST, preferred_element_type=jnp.float32)


def lane_of(shape):
    return lax.broadcasted_iota(jnp.int32, shape, len(shape) - 1)


def swap_halves(x):
    return pltpu.roll(x, x.shape[1] // 2, axis=1)


def pack(x):
    n = x.shape[0] // 2
    return jnp.where(lane_of((n, x.shape[1])) < x.shape[1] // 2, x[:n], x[n:])


def unpack(x):
    other = swap_halves(x)
    left = lane_of(x.shape) < x.shape[1] // 2
    return jnp.concatenate([jnp.where(left, x, other), jnp.where(left, other, x)], axis=0)


def gram_doubled(x, rank):
    return dot_f32(x.T, x)[:rank]


def diag_mask(rank, wide):
    rows = lax.broadcasted_iota(jnp.int32, (rank, wide), 0)
    lanes = lane_of((rank, wide))
    return (lanes == rows) | (lanes == rows + rank)


def col_scale(raw_gram, total):
    diag = jnp.where(diag_mask(*raw_gram.shape), raw_gram, 0.0)
    return jnp.sqrt(jnp.sum(diag, axis=0, keepdims=True) / total + EPSILON)


def balance(system):
    diag = jnp.where(diag_mask(*system.shape), system, 0.0)
    by_lane = lax.rsqrt(jnp.sum(diag, axis=0, keepdims=True))
    by_sub = lax.rsqrt(0.5 * jnp.sum(diag, axis=1, keepdims=True))
    return system * by_sub * by_lane, by_lane, by_sub


def sweep_blocks(a, count):
    rank, wide = a.shape
    tiles = rank // PANEL
    tile = (PANEL, wide)
    lane = lane_of(tile) % rank
    sub = lax.broadcasted_iota(jnp.int32, tile, 0)

    def row(x, p):
        return jnp.broadcast_to(x[p : p + 1], tile)

    def block(_, a):
        head, rest = a[:PANEL], a[PANEL:].reshape(tiles - 1, PANEL, wide)
        cols = [jnp.broadcast_to(head[:, q : q + 1], tile) for q in range(PANEL)]
        for p in range(0, PANEL, 2):
            u, v = cols[p], cols[p + 1]
            uu, uv, vv = row(u, p), row(u, p + 1), row(v, p + 1)
            inv = 1.0 / (uu * vv - uv * uv)
            iu, iv, ic = vv * inv, uu * inv, -(uv * inv)

            def reduced(x):
                x0, x1 = row(x, p), row(x, p + 1)
                return iu * x0 + ic * x1, ic * x0 + iv * x1

            def put(x, top, low):
                new = x - u * top - v * low
                return jnp.where(sub == p, top, jnp.where(sub == p + 1, low, new))

            for q in range(p + 2, PANEL):
                cols[q] = put(cols[q], *reduced(cols[q]))
            top, low = reduced(head)
            at_u, at_v = lane == p, lane == p + 1
            top = jnp.where(at_u, -iu, jnp.where(at_v, -ic, top))
            low = jnp.where(at_u, -ic, jnp.where(at_v, -iv, low))
            head = put(jnp.where(at_u | at_v, 0.0, head), top, low)
        new = jnp.where((lane < PANEL)[None], 0.0, rest)
        for q in range(PANEL):
            new = new - jnp.broadcast_to(rest[:, :, q : q + 1], rest.shape) * row(head, q)
        a = jnp.concatenate([new.reshape(rank - PANEL, wide), head], axis=0)
        return pltpu.roll(a, wide - PANEL, axis=1)

    return lax.fori_loop(0, count, block, a)


def solve_packed(packed, minus_inv):
    wide = minus_inv.shape[1]
    inv = -minus_inv
    zero = jnp.zeros_like(inv)
    both = jnp.concatenate(
        [jnp.concatenate([inv, zero], axis=1), jnp.concatenate([zero, inv], axis=1)], axis=0
    )
    out = dot_f32(packed, both)
    return jnp.concatenate([out[:, :wide], out[:, wide:]], axis=0)


def split_weights(x):
    high = x.astype(jnp.bfloat16).astype(jnp.float32)
    mixed = jnp.where(lane_of(x.shape) < x.shape[1] // 2, high, x - high).astype(jnp.bfloat16)
    return jnp.concatenate([mixed, mixed], axis=0)


def kernel(
    nr,
    nc,
    tensor_in,
    second_in,
    third_in,
    first_out,
    second_out,
    third_out,
    tensor,
    by_row,
    by_col,
    contracted,
    weights,
    first_d,
    second_d,
    third_d,
    third_raw,
    third_inv,
    scale2_row,
    gram2,
    gram3,
    m3_rows,
    m1_buf,
    g1_src,
    g1_buf,
    g1_all,
    m2_src,
    m2_buf,
    m2_all,
    g2_buf,
    m3_buf,
    m3_all,
    col_send,
    col_recv,
    row_send,
    row_recv,
    load_sem,
):
    K, I, J = tensor.shape
    R = second_in.shape[0]
    my_row = lax.axis_index("rows")
    my_col = lax.axis_index("cols")

    def col_peer(d):
        return lax.rem(my_col + d, nc)

    def row_peer(d):
        return lax.rem(my_row + d, nr)

    def col_copies(kind, buf):
        return [
            pltpu.make_async_remote_copy(
                src_ref=buf.at[my_col],
                dst_ref=buf.at[my_col],
                send_sem=col_send.at[kind, d - 1],
                recv_sem=col_recv.at[kind, d - 1],
                device_id=(my_row, col_peer(d)),
                device_id_type=MESH,
            )
            for d in range(1, nc)
        ]

    def row_copies(kind, src, dst, scatter=False):
        return [
            pltpu.make_async_remote_copy(
                src_ref=src.at[row_peer(d)] if scatter else src.at[my_row],
                dst_ref=dst.at[my_row],
                send_sem=row_send.at[kind, d - 1],
                recv_sem=row_recv.at[kind, d - 1],
                device_id=(row_peer(d), my_col),
                device_id_type=MESH,
            )
            for d in range(1, nr)
        ]

    def start(copies):
        for copy in copies:
            copy.start()
        return copies

    def wait(copies):
        for copy in copies:
            copy.wait()

    def total(buf, n):
        out = buf[0]
        for s in range(1, n):
            out = out + buf[s]
        return out

    def joined(buf, n):
        return jnp.concatenate([buf[s] for s in range(n)], axis=0)

    barrier = pltpu.get_barrier_semaphore()
    for d in range(1, nc):
        pl.semaphore_signal(barrier, inc=1, device_id=(my_row, col_peer(d)), device_id_type=MESH)
    for d in range(1, nr):
        pl.semaphore_signal(barrier, inc=1, device_id=(row_peer(d), my_col), device_id_type=MESH)

    GROUP = 8
    loads = [
        pltpu.make_async_copy(
            tensor_in.at[pl.ds(g * GROUP, GROUP)], tensor.at[pl.ds(g * GROUP, GROUP)], load_sem.at[g]
        )
        for g in range(K // GROUP)
    ]
    start(loads)
    start_second = second_in[...]
    start_second = jnp.concatenate([start_second, start_second], axis=0).T
    start_third = third_in[...]
    start_third = jnp.concatenate([start_third, start_third], axis=1)
    g2_buf[my_col] = pack(gram_doubled(start_second, R))
    pl.semaphore_wait(barrier, nc - 1 + nr - 1)
    copies = start(col_copies(1, g2_buf))

    def settle_third(third):
        inv_norm = 1.0 / jnp.sqrt(jnp.sum(third * third, axis=0, keepdims=True))
        unit = third * inv_norm
        third_d[...] = unit
        third_inv[...] = inv_norm
        gram3[...] = gram_doubled(unit, R)

    settle_third(start_third)

    def split_slice(k, _):
        rows = pl.ds(pl.multiple_of(k * I, I), I)
        block = tensor[k]
        high = block.astype(jnp.bfloat16)
        by_row[rows, :J] = high
        by_row[rows, J:] = (block - high.astype(jnp.float32)).astype(jnp.bfloat16)
        turned = block.T
        rows = pl.ds(pl.multiple_of(k * J, J), J)
        high = turned.astype(jnp.bfloat16)
        by_col[rows, :I] = high
        by_col[rows, I:] = (turned - high.astype(jnp.float32)).astype(jnp.bfloat16)
        return 0

    for g, load in enumerate(loads):
        load.wait()
        lax.fori_loop(g * GROUP, (g + 1) * GROUP, split_slice, 0)
    wait(copies)
    gram = unpack(total(g2_buf, nc))
    gram2[...] = gram
    scale = col_scale(gram, J * nc)
    scale2_row[...] = scale
    second_d[...] = start_second / scale

    def contract(source, extent, keep):
        def step(o, acc):
            rows = pl.ds(pl.multiple_of(o * GROUP * extent, GROUP * extent), GROUP * extent)
            part = jnp.dot(source[rows, :], weights[...], preferred_element_type=jnp.float32)
            for u in range(GROUP):
                k = o * GROUP + u
                one = part[u * extent : (u + 1) * extent]
                if keep:
                    contracted[k] = one
                acc = acc + one * third_d[pl.ds(k, 1), :]
            return acc

        acc = lax.fori_loop(0, K // GROUP, step, jnp.zeros((extent, 2 * R), jnp.float32))
        return acc + swap_halves(acc)

    BLOCKS = R // PANEL

    def sweep(_, carry):
        weights[...] = split_weights(second_d[...])
        m1_buf[my_col] = pack(contract(by_row, I, False))
        m1_copies = start(col_copies(0, m1_buf))
        system, by_lane, _ = balance(gram3[...] * gram2[...])
        inv = sweep_blocks(system, BLOCKS)
        around = by_lane * scale2_row[...]
        wait(m1_copies)
        raw1 = solve_packed(total(m1_buf, nc) * around, inv) * (around * third_inv[...])

        packed = pack(gram_doubled(raw1, R))
        share = packed.shape[0] // nc
        for c in range(nc):
            g1_src[c] = packed[c * share : (c + 1) * share]
        g1_buf[my_row] = g1_src[my_col]
        g1_copies = start(row_copies(0, g1_buf, g1_buf))
        weights[...] = split_weights(raw1)
        packed = pack(contract(by_col, J, True))
        share = packed.shape[0] // nr
        for r in range(nr):
            m2_src[r] = packed[r * share : (r + 1) * share]
        m2_buf[my_row] = m2_src[my_row]
        m2_copies = start(row_copies(1, m2_src, m2_buf, scatter=True))
        wait(g1_copies)
        g1_all[my_col] = total(g1_buf, nr)
        g1_copies = start(col_copies(2, g1_all))
        wait(m2_copies)
        m2_all[my_row] = total(m2_buf, nr)
        m2_copies = start(row_copies(2, m2_all, m2_all))
        wait(g1_copies)

        gram1 = unpack(joined(g1_all, nc))
        system, by_lane1, by_sub1 = balance(gram3[...] * gram1)
        inv = sweep_blocks(system, BLOCKS)
        gram1 = gram1 * by_sub1 * by_lane1
        scale1 = col_scale(unpack(joined(g1_all, nc)), I * nr)
        first_d[...] = raw1 / scale1
        wait(m2_copies)
        raw2 = solve_packed(joined(m2_all, nr) * by_lane1, inv) * (by_lane1 * scale1)
        g2_buf[my_col] = pack(gram_doubled(raw2, R))
        g2_copies = start(col_copies(1, g2_buf))

        scaled = raw2 / scale1
        for k in range(K):
            m3_rows[k : k + 1] = jnp.sum(contracted[k] * scaled, axis=0, keepdims=True)
        m3 = m3_rows[...]
        m3_buf[my_row] = pack(m3 + swap_halves(m3))
        m3_copies = start(row_copies(3, m3_buf, m3_buf))
        wait(g2_copies)
        gram = unpack(total(g2_buf, nc))
        gram2[...] = gram
        system, by_lane, _ = balance(gram1 * gram)
        inv = sweep_blocks(system, BLOCKS // 2)
        wait(m3_copies)
        m3_all[my_col] = total(m3_buf, nr)
        m3_copies = start(col_copies(3, m3_all))
        inv = sweep_blocks(inv, BLOCKS - BLOCKS // 2)
        scale2 = col_scale(gram, J * nc)
        scale2_row[...] = scale2
        second_d[...] = raw2 / scale2
        around = by_lane * by_lane1 * scale1
        wait(m3_copies)
        third = solve_packed(total(m3_all, nc) * around, inv) * (around * scale2)
        third_raw[...] = third
        settle_third(third)
        return carry

    lax.fori_loop(0, ITERS, sweep, 0)
    first_out[...] = first_d[:, :R]
    second_out[...] = second_d[:, :R]
    third_out[...] = third_raw[:, :R]


def per_device(nr, nc, tensor, second_init, third_init):
    K, I, J = tensor.shape
    R = second_init.shape[1]
    wide = 2 * R
    f32 = jnp.float32
    half = R // 2

    def vmem(*shape):
        return pltpu.VMEM(shape, f32)

    return pl.pallas_call(
        functools.partial(kernel, nr, nc),
        out_shape=(
            jax.ShapeDtypeStruct((I, R), f32),
            jax.ShapeDtypeStruct((J, R), f32),
            jax.ShapeDtypeStruct((K, R), f32),
        ),
        in_specs=[pl.BlockSpec(memory_space=pl.ANY)] + [pl.BlockSpec(memory_space=pltpu.VMEM)] * 2,
        out_specs=(pl.BlockSpec(memory_space=pltpu.VMEM),) * 3,
        scratch_shapes=[
            vmem(K, I, J),
            pltpu.VMEM((K * I, 2 * J), jnp.bfloat16),
            pltpu.VMEM((K * J, 2 * I), jnp.bfloat16),
            vmem(K, J, wide),
            pltpu.VMEM((2 * J, wide), jnp.bfloat16),
            vmem(I, wide),
            vmem(J, wide),
            vmem(K, wide),
            vmem(K, wide),
            vmem(1, wide),
            vmem(1, wide),
            vmem(R, wide),
            vmem(R, wide),
            vmem(K, wide),
            vmem(nc, I // 2, wide),
            vmem(nc, half // nc, wide),
            vmem(nr, half // nc, wide),
            vmem(nc, half // nc, wide),
            vmem(nr, J // 2 // nr, wide),
            vmem(nr, J // 2 // nr, wide),
            vmem(nr, J // 2 // nr, wide),
            vmem(nc, half, wide),
            vmem(nr, K // 2, wide),
            vmem(nc, K // 2, wide),
            pltpu.SemaphoreType.DMA((4, nc - 1)),
            pltpu.SemaphoreType.DMA((4, nc - 1)),
            pltpu.SemaphoreType.DMA((4, nr - 1)),
            pltpu.SemaphoreType.DMA((4, nr - 1)),
            pltpu.SemaphoreType.DMA((K // 8,)),
        ],
        compiler_params=pltpu.CompilerParams(
            collective_id=0, has_side_effects=True, vmem_limit_bytes=56 * 1024 * 1024
        ),
        cost_estimate=pl.CostEstimate(
            flops=ITERS * 2 * 2 * K * I * J * 2 * wide, bytes_accessed=4 * K * I * J, transcendentals=0
        ),
        name="als_sweeps",
    )(tensor, second_init.T, third_init)


def solution(mesh):
    return jax.shard_map(
        functools.partial(per_device, mesh.shape["rows"], mesh.shape["cols"]),
        mesh=mesh,
        in_specs=(P(None, "rows", "cols"), P("cols", None), P()),
        out_specs=(P("rows", None), P("cols", None), P()),
        check_vma=False,
    )
```

```python
import functools

import jax
import jax.numpy as jnp
from jax import lax
from jax.experimental import pallas as pl
from jax.experimental.pallas import tpu as pltpu
from jax.sharding import PartitionSpec as P

ITERS = 5
EPSILON = 1e-05
MESH = pl.DeviceIdType.MESH
PANEL = 8


def lane_of(shape):
    return lax.broadcasted_iota(jnp.int32, shape, len(shape) - 1)


def swap_halves(x):
    return pltpu.roll(x, x.shape[1] // 2, axis=1)


def pack(x):
    n = x.shape[0] // 2
    return jnp.where(lane_of((n, x.shape[1])) < x.shape[1] // 2, x[:n], x[n:])


def unpack(x):
    other = swap_halves(x)
    left = lane_of(x.shape) < x.shape[1] // 2
    return jnp.concatenate([jnp.where(left, x, other), jnp.where(left, other, x)], axis=0)


def split_halves(x):
    high = x.astype(jnp.bfloat16).astype(jnp.float32)
    return jnp.where(lane_of(x.shape) < x.shape[1] // 2, high, x - high).astype(jnp.bfloat16)


def gram_doubled(x, rank):
    left = split_halves(x)
    high = x.T.astype(jnp.bfloat16).astype(jnp.float32)
    parts = x.T - high
    rows = lax.broadcasted_iota(jnp.int32, parts.shape, 0)
    turned = jnp.where(rows < rank, high, parts).astype(jnp.bfloat16)
    all_four = jnp.dot(turned, left, preferred_element_type=jnp.float32)
    both = all_four[:rank] + all_four[rank:]
    return both + swap_halves(both)


def diag_mask(rank, wide):
    rows = lax.broadcasted_iota(jnp.int32, (rank, wide), 0)
    lanes = lane_of((rank, wide))
    return (lanes == rows) | (lanes == rows + rank)


def col_scale(raw_gram, total):
    diag = jnp.where(diag_mask(*raw_gram.shape), raw_gram, 0.0)
    return jnp.sqrt(jnp.sum(diag, axis=0, keepdims=True) / total + EPSILON)


def balance(system):
    diag = jnp.where(diag_mask(*system.shape), system, 0.0)
    by_lane = lax.rsqrt(jnp.sum(diag, axis=0, keepdims=True))
    by_sub = lax.rsqrt(0.5 * jnp.sum(diag, axis=1, keepdims=True))
    return system * by_sub * by_lane, by_lane, by_sub


def sweep_blocks(a, count):
    rank, wide = a.shape
    tiles = rank // PANEL
    tile = (PANEL, wide)
    lane = lane_of(tile) % rank
    sub = lax.broadcasted_iota(jnp.int32, tile, 0)

    def row(x, p):
        return jnp.broadcast_to(x[p : p + 1], tile)

    def block(_, a):
        head, rest = a[:PANEL], a[PANEL:].reshape(tiles - 1, PANEL, wide)
        cols = [jnp.broadcast_to(head[:, q : q + 1], tile) for q in range(PANEL)]
        for p in range(0, PANEL, 2):
            u, v = cols[p], cols[p + 1]
            uu, uv, vv = row(u, p), row(u, p + 1), row(v, p + 1)
            inv = 1.0 / (uu * vv - uv * uv)
            iu, iv, ic = vv * inv, uu * inv, -(uv * inv)

            def reduced(x):
                x0, x1 = row(x, p), row(x, p + 1)
                return iu * x0 + ic * x1, ic * x0 + iv * x1

            def put(x, top, low):
                new = x - u * top - v * low
                return jnp.where(sub == p, top, jnp.where(sub == p + 1, low, new))

            for q in range(p + 2, PANEL):
                cols[q] = put(cols[q], *reduced(cols[q]))
            top, low = reduced(head)
            at_u, at_v = lane == p, lane == p + 1
            top = jnp.where(at_u, -iu, jnp.where(at_v, -ic, top))
            low = jnp.where(at_u, -ic, jnp.where(at_v, -iv, low))
            head = put(jnp.where(at_u | at_v, 0.0, head), top, low)
        new = jnp.where((lane < PANEL)[None], 0.0, rest)
        for q in range(PANEL):
            new = new - jnp.broadcast_to(rest[:, :, q : q + 1], rest.shape) * row(head, q)
        a = jnp.concatenate([new.reshape(rank - PANEL, wide), head], axis=0)
        return pltpu.roll(a, wide - PANEL, axis=1)

    return lax.fori_loop(0, count, block, a)


def solve_packed(packed, minus_inv):
    parts = split_halves(-minus_inv)
    weights = jnp.concatenate([parts, parts], axis=0)
    out = jnp.dot(split_halves(unpack(packed)), weights, preferred_element_type=jnp.float32)
    return out + swap_halves(out)


def split_weights(x):
    mixed = split_halves(x)
    return jnp.concatenate([mixed, mixed], axis=0)


def kernel(
    nr,
    nc,
    tensor,
    second_in,
    third_in,
    first_out,
    second_out,
    third_out,
    by_row,
    by_col,
    contracted,
    weights,
    first_d,
    second_d,
    third_d,
    third_raw,
    third_inv,
    scale2_row,
    gram2,
    gram3,
    m3_rows,
    m1_buf,
    g1_src,
    g1_buf,
    g1_all,
    m2_src,
    m2_buf,
    m2_all,
    g2_buf,
    m3_buf,
    m3_all,
    col_send,
    col_recv,
    row_send,
    row_recv,
):
    K, I, J = tensor.shape
    R = second_in.shape[0]
    my_row = lax.axis_index("rows")
    my_col = lax.axis_index("cols")

    def col_peer(d):
        return lax.rem(my_col + d, nc)

    def row_peer(d):
        return lax.rem(my_row + d, nr)

    def col_copies(kind, buf):
        return [
            pltpu.make_async_remote_copy(
                src_ref=buf.at[my_col],
                dst_ref=buf.at[my_col],
                send_sem=col_send.at[kind, d - 1],
                recv_sem=col_recv.at[kind, d - 1],
                device_id=(my_row, col_peer(d)),
                device_id_type=MESH,
            )
            for d in range(1, nc)
        ]

    def row_copies(kind, src, dst, scatter=False):
        return [
            pltpu.make_async_remote_copy(
                src_ref=src.at[row_peer(d)] if scatter else src.at[my_row],
                dst_ref=dst.at[my_row],
                send_sem=row_send.at[kind, d - 1],
                recv_sem=row_recv.at[kind, d - 1],
                device_id=(row_peer(d), my_col),
                device_id_type=MESH,
            )
            for d in range(1, nr)
        ]

    def start(copies):
        for copy in copies:
            copy.start()
        return copies

    def wait(copies):
        for copy in copies:
            copy.wait()

    def total(buf, n):
        out = buf[0]
        for s in range(1, n):
            out = out + buf[s]
        return out

    def joined(buf, n):
        return jnp.concatenate([buf[s] for s in range(n)], axis=0)

    barrier = pltpu.get_barrier_semaphore()
    for d in range(1, nc):
        pl.semaphore_signal(barrier, inc=1, device_id=(my_row, col_peer(d)), device_id_type=MESH)
    for d in range(1, nr):
        pl.semaphore_signal(barrier, inc=1, device_id=(row_peer(d), my_col), device_id_type=MESH)

    GROUP = 8
    start_second = second_in[...]
    start_second = jnp.concatenate([start_second, start_second], axis=0).T
    start_third = third_in[...]
    start_third = jnp.concatenate([start_third, start_third], axis=1)
    g2_buf[my_col] = pack(gram_doubled(start_second, R))
    pl.semaphore_wait(barrier, nc - 1 + nr - 1)
    copies = start(col_copies(1, g2_buf))

    def settle_third(third):
        inv_norm = 1.0 / jnp.sqrt(jnp.sum(third * third, axis=0, keepdims=True))
        unit = third * inv_norm
        third_d[...] = unit
        third_inv[...] = inv_norm
        gram3[...] = gram_doubled(unit, R)

    settle_third(start_third)

    def split_slice(k, _):
        rows = pl.ds(pl.multiple_of(k * I, I), I)
        block = tensor[k]
        high = block.astype(jnp.bfloat16)
        by_row[rows, :J] = high
        by_row[rows, J:] = (block - high.astype(jnp.float32)).astype(jnp.bfloat16)
        turned = block.T
        rows = pl.ds(pl.multiple_of(k * J, J), J)
        high = turned.astype(jnp.bfloat16)
        by_col[rows, :I] = high
        by_col[rows, I:] = (turned - high.astype(jnp.float32)).astype(jnp.bfloat16)
        return 0

    lax.fori_loop(0, K, split_slice, 0)
    wait(copies)
    gram = unpack(total(g2_buf, nc))
    gram2[...] = gram
    scale = col_scale(gram, J * nc)
    scale2_row[...] = scale
    second_d[...] = start_second / scale

    def contract(source, extent, keep):
        def step(o, acc):
            rows = pl.ds(pl.multiple_of(o * GROUP * extent, GROUP * extent), GROUP * extent)
            part = jnp.dot(source[rows, :], weights[...], preferred_element_type=jnp.float32)
            for u in range(GROUP):
                k = o * GROUP + u
                one = part[u * extent : (u + 1) * extent]
                if keep:
                    contracted[k] = one
                acc = acc + one * third_d[pl.ds(k, 1), :]
            return acc

        acc = lax.fori_loop(0, K // GROUP, step, jnp.zeros((extent, 2 * R), jnp.float32))
        return acc + swap_halves(acc)

    BLOCKS = R // PANEL

    def sweep(_, carry):
        weights[...] = split_weights(second_d[...])
        m1_buf[my_col] = pack(contract(by_row, I, False))
        m1_copies = start(col_copies(0, m1_buf))
        system, by_lane, _ = balance(gram3[...] * gram2[...])
        inv = sweep_blocks(system, BLOCKS)
        around = by_lane * scale2_row[...]
        wait(m1_copies)
        raw1 = solve_packed(total(m1_buf, nc) * around, inv) * (around * third_inv[...])

        packed = pack(gram_doubled(raw1, R))
        share = packed.shape[0] // nc
        for c in range(nc):
            g1_src[c] = packed[c * share : (c + 1) * share]
        g1_buf[my_row] = g1_src[my_col]
        g1_copies = start(row_copies(0, g1_buf, g1_buf))
        weights[...] = split_weights(raw1)
        packed = pack(contract(by_col, J, True))
        share = packed.shape[0] // nr
        for r in range(nr):
            m2_src[r] = packed[r * share : (r + 1) * share]
        m2_buf[my_row] = m2_src[my_row]
        m2_copies = start(row_copies(1, m2_src, m2_buf, scatter=True))
        wait(g1_copies)
        g1_all[my_col] = total(g1_buf, nr)
        g1_copies = start(col_copies(2, g1_all))
        wait(m2_copies)
        m2_all[my_row] = total(m2_buf, nr)
        m2_copies = start(row_copies(2, m2_all, m2_all))
        wait(g1_copies)

        gram1 = unpack(joined(g1_all, nc))
        system, by_lane1, by_sub1 = balance(gram3[...] * gram1)
        inv = sweep_blocks(system, BLOCKS)
        gram1 = gram1 * by_sub1 * by_lane1
        scale1 = col_scale(unpack(joined(g1_all, nc)), I * nr)
        first_d[...] = raw1 / scale1
        wait(m2_copies)
        raw2 = solve_packed(joined(m2_all, nr) * by_lane1, inv) * (by_lane1 * scale1)
        g2_buf[my_col] = pack(gram_doubled(raw2, R))
        g2_copies = start(col_copies(1, g2_buf))

        scaled = raw2 / scale1
        for k in range(K):
            m3_rows[k : k + 1] = jnp.sum(contracted[k] * scaled, axis=0, keepdims=True)
        m3 = m3_rows[...]
        m3_buf[my_row] = pack(m3 + swap_halves(m3))
        m3_copies = start(row_copies(3, m3_buf, m3_buf))
        wait(g2_copies)
        gram = unpack(total(g2_buf, nc))
        gram2[...] = gram
        system, by_lane, _ = balance(gram1 * gram)
        inv = sweep_blocks(system, BLOCKS // 2)
        wait(m3_copies)
        m3_all[my_col] = total(m3_buf, nr)
        m3_copies = start(col_copies(3, m3_all))
        inv = sweep_blocks(inv, BLOCKS - BLOCKS // 2)
        scale2 = col_scale(gram, J * nc)
        scale2_row[...] = scale2
        second_d[...] = raw2 / scale2
        around = by_lane * by_lane1 * scale1
        wait(m3_copies)
        third = solve_packed(total(m3_all, nc) * around, inv) * (around * scale2)
        third_raw[...] = third
        settle_third(third)
        return carry

    lax.fori_loop(0, ITERS, sweep, 0)
    first_out[...] = first_d[:, :R]
    second_out[...] = second_d[:, :R]
    third_out[...] = third_raw[:, :R]


def per_device(nr, nc, tensor, second_init, third_init):
    K, I, J = tensor.shape
    R = second_init.shape[1]
    wide = 2 * R
    f32 = jnp.float32
    half = R // 2

    def vmem(*shape):
        return pltpu.VMEM(shape, f32)

    return pl.pallas_call(
        functools.partial(kernel, nr, nc),
        out_shape=(
            jax.ShapeDtypeStruct((I, R), f32),
            jax.ShapeDtypeStruct((J, R), f32),
            jax.ShapeDtypeStruct((K, R), f32),
        ),
        in_specs=[pl.BlockSpec(memory_space=pltpu.VMEM)] * 3,
        out_specs=(pl.BlockSpec(memory_space=pltpu.VMEM),) * 3,
        scratch_shapes=[
            pltpu.VMEM((K * I, 2 * J), jnp.bfloat16),
            pltpu.VMEM((K * J, 2 * I), jnp.bfloat16),
            vmem(K, J, wide),
            pltpu.VMEM((2 * J, wide), jnp.bfloat16),
            vmem(I, wide),
            vmem(J, wide),
            vmem(K, wide),
            vmem(K, wide),
            vmem(1, wide),
            vmem(1, wide),
            vmem(R, wide),
            vmem(R, wide),
            vmem(K, wide),
            vmem(nc, I // 2, wide),
            vmem(nc, half // nc, wide),
            vmem(nr, half // nc, wide),
            vmem(nc, half // nc, wide),
            vmem(nr, J // 2 // nr, wide),
            vmem(nr, J // 2 // nr, wide),
            vmem(nr, J // 2 // nr, wide),
            vmem(nc, half, wide),
            vmem(nr, K // 2, wide),
            vmem(nc, K // 2, wide),
            pltpu.SemaphoreType.DMA((4, nc - 1)),
            pltpu.SemaphoreType.DMA((4, nc - 1)),
            pltpu.SemaphoreType.DMA((4, nr - 1)),
            pltpu.SemaphoreType.DMA((4, nr - 1)),
        ],
        compiler_params=pltpu.CompilerParams(
            collective_id=0, has_side_effects=True, vmem_limit_bytes=32 * 1024 * 1024
        ),
        cost_estimate=pl.CostEstimate(
            flops=ITERS * 2 * 2 * K * I * J * 2 * wide, bytes_accessed=4 * K * I * J, transcendentals=0
        ),
        name="als_sweeps",
    )(tensor, second_init.T, third_init)


def solution(mesh):
    return jax.shard_map(
        functools.partial(per_device, mesh.shape["rows"], mesh.shape["cols"]),
        mesh=mesh,
        in_specs=(P(None, "rows", "cols"), P("cols", None), P()),
        out_specs=(P("rows", None), P("cols", None), P()),
        check_vma=False,
    )
```

```python
import functools

import jax
import jax.numpy as jnp
from jax import lax
from jax.experimental import pallas as pl
from jax.experimental.pallas import tpu as pltpu
from jax.sharding import PartitionSpec as P

ITERS = 5
EPSILON = 1e-05
MESH = pl.DeviceIdType.MESH
PANEL = 8


def lane_of(shape):
    return lax.broadcasted_iota(jnp.int32, shape, len(shape) - 1)


def swap_halves(x):
    return pltpu.roll(x, x.shape[1] // 2, axis=1)


def pack(x):
    n = x.shape[0] // 2
    return jnp.where(lane_of((n, x.shape[1])) < x.shape[1] // 2, x[:n], x[n:])


def unpack(x):
    other = swap_halves(x)
    left = lane_of(x.shape) < x.shape[1] // 2
    return jnp.concatenate([jnp.where(left, x, other), jnp.where(left, other, x)], axis=0)


def split_halves(x):
    high = x.astype(jnp.bfloat16).astype(jnp.float32)
    return jnp.where(lane_of(x.shape) < x.shape[1] // 2, high, x - high).astype(jnp.bfloat16)


def gram_doubled(x, rank):
    left = split_halves(x)
    high = x.T.astype(jnp.bfloat16).astype(jnp.float32)
    parts = x.T - high
    rows = lax.broadcasted_iota(jnp.int32, parts.shape, 0)
    turned = jnp.where(rows < rank, high, parts).astype(jnp.bfloat16)
    all_four = jnp.dot(turned, left, preferred_element_type=jnp.float32)
    both = all_four[:rank] + all_four[rank:]
    return both + swap_halves(both)


def diag_mask(rank, wide):
    rows = lax.broadcasted_iota(jnp.int32, (rank, wide), 0)
    lanes = lane_of((rank, wide))
    return (lanes == rows) | (lanes == rows + rank)


def col_scale(raw_gram, total):
    diag = jnp.where(diag_mask(*raw_gram.shape), raw_gram, 0.0)
    return jnp.sqrt(jnp.sum(diag, axis=0, keepdims=True) / total + EPSILON)


def balance(system):
    diag = jnp.where(diag_mask(*system.shape), system, 0.0)
    by_lane = lax.rsqrt(jnp.sum(diag, axis=0, keepdims=True))
    by_sub = lax.rsqrt(0.5 * jnp.sum(diag, axis=1, keepdims=True))
    return system * by_sub * by_lane, by_lane, by_sub


def sweep_blocks(a, count):
    rank, wide = a.shape
    tiles = rank // PANEL
    tile = (PANEL, wide)
    lane = lane_of(tile) % rank
    sub = lax.broadcasted_iota(jnp.int32, tile, 0)

    def row(x, p):
        return jnp.broadcast_to(x[p : p + 1], tile)

    def block(_, a):
        head, rest = a[:PANEL], a[PANEL:].reshape(tiles - 1, PANEL, wide)
        cols = [jnp.broadcast_to(head[:, q : q + 1], tile) for q in range(PANEL)]
        for p in range(0, PANEL, 2):
            u, v = cols[p], cols[p + 1]
            uu, uv, vv = row(u, p), row(u, p + 1), row(v, p + 1)
            inv = 1.0 / (uu * vv - uv * uv)
            iu, iv, ic = vv * inv, uu * inv, -(uv * inv)

            def reduced(x):
                x0, x1 = row(x, p), row(x, p + 1)
                return iu * x0 + ic * x1, ic * x0 + iv * x1

            def put(x, top, low):
                new = x - u * top - v * low
                return jnp.where(sub == p, top, jnp.where(sub == p + 1, low, new))

            for q in range(p + 2, PANEL):
                cols[q] = put(cols[q], *reduced(cols[q]))
            top, low = reduced(head)
            at_u, at_v = lane == p, lane == p + 1
            top = jnp.where(at_u, -iu, jnp.where(at_v, -ic, top))
            low = jnp.where(at_u, -ic, jnp.where(at_v, -iv, low))
            head = put(jnp.where(at_u | at_v, 0.0, head), top, low)
        new = jnp.where((lane < PANEL)[None], 0.0, rest)
        for q in range(PANEL):
            new = new - jnp.broadcast_to(rest[:, :, q : q + 1], rest.shape) * row(head, q)
        a = jnp.concatenate([new.reshape(rank - PANEL, wide), head], axis=0)
        return pltpu.roll(a, wide - PANEL, axis=1)

    return lax.fori_loop(0, count, block, a)


def solve_packed(packed, minus_inv):
    parts = split_halves(-minus_inv)
    weights = jnp.concatenate([parts, parts], axis=0)
    out = jnp.dot(split_halves(unpack(packed)), weights, preferred_element_type=jnp.float32)
    return out + swap_halves(out)


def split_weights(x):
    mixed = split_halves(x)
    return jnp.concatenate([mixed, mixed], axis=0)


def kernel(
    nr,
    nc,
    tensor,
    second_in,
    third_in,
    first_out,
    second_out,
    third_out,
    by_row,
    by_col,
    contracted,
    weights,
    first_d,
    second_d,
    third_d,
    third_raw,
    third_inv,
    scale2_row,
    gram2,
    gram3,
    m3_rows,
    m1_buf,
    g1_src,
    g1_buf,
    g1_all,
    m2_src,
    m2_buf,
    m2_all,
    g2_buf,
    m3_buf,
    m3_all,
    col_send,
    col_recv,
    row_send,
    row_recv,
):
    K, I, J = tensor.shape
    R = second_in.shape[0]
    my_row = lax.axis_index("rows")
    my_col = lax.axis_index("cols")

    def col_peer(d):
        return lax.rem(my_col + d, nc)

    def row_peer(d):
        return lax.rem(my_row + d, nr)

    def col_copies(kind, buf):
        return [
            pltpu.make_async_remote_copy(
                src_ref=buf.at[my_col],
                dst_ref=buf.at[my_col],
                send_sem=col_send.at[kind, d - 1],
                recv_sem=col_recv.at[kind, d - 1],
                device_id=(my_row, col_peer(d)),
                device_id_type=MESH,
            )
            for d in range(1, nc)
        ]

    def row_copies(kind, src, dst, scatter=False):
        return [
            pltpu.make_async_remote_copy(
                src_ref=src.at[row_peer(d)] if scatter else src.at[my_row],
                dst_ref=dst.at[my_row],
                send_sem=row_send.at[kind, d - 1],
                recv_sem=row_recv.at[kind, d - 1],
                device_id=(row_peer(d), my_col),
                device_id_type=MESH,
            )
            for d in range(1, nr)
        ]

    def start(copies):
        for copy in copies:
            copy.start()
        return copies

    def wait(copies):
        for copy in copies:
            copy.wait()

    def total(buf, n):
        out = buf[0]
        for s in range(1, n):
            out = out + buf[s]
        return out

    def joined(buf, n):
        return jnp.concatenate([buf[s] for s in range(n)], axis=0)

    barrier = pltpu.get_barrier_semaphore()
    for d in range(1, nc):
        pl.semaphore_signal(barrier, inc=1, device_id=(my_row, col_peer(d)), device_id_type=MESH)
    for d in range(1, nr):
        pl.semaphore_signal(barrier, inc=1, device_id=(row_peer(d), my_col), device_id_type=MESH)

    GROUP = 8
    start_second = second_in[...]
    start_second = jnp.concatenate([start_second, start_second], axis=0).T
    start_third = third_in[...]
    start_third = jnp.concatenate([start_third, start_third], axis=1)
    g2_buf[my_col] = pack(gram_doubled(start_second, R))
    pl.semaphore_wait(barrier, nc - 1 + nr - 1)
    copies = start(col_copies(1, g2_buf))

    def settle_third(third):
        inv_norm = 1.0 / jnp.sqrt(jnp.sum(third * third, axis=0, keepdims=True))
        unit = third * inv_norm
        third_d[...] = unit
        third_inv[...] = inv_norm
        gram3[...] = gram_doubled(unit, R)

    settle_third(start_third)

    def split_slice(k, _):
        rows = pl.ds(pl.multiple_of(k * I, I), I)
        block = tensor[k]
        high = block.astype(jnp.bfloat16)
        by_row[rows, :J] = high
        by_row[rows, J:] = (block - high.astype(jnp.float32)).astype(jnp.bfloat16)
        turned = block.T
        rows = pl.ds(pl.multiple_of(k * J, J), J)
        high = turned.astype(jnp.bfloat16)
        by_col[rows, :I] = high
        by_col[rows, I:] = (turned - high.astype(jnp.float32)).astype(jnp.bfloat16)
        return 0

    lax.fori_loop(0, K, split_slice, 0)
    wait(copies)
    gram = unpack(total(g2_buf, nc))
    gram2[...] = gram
    scale = col_scale(gram, J * nc)
    scale2_row[...] = scale
    second_d[...] = start_second / scale

    def contract(source, extent, keep):
        def step(o, acc):
            for u in range(GROUP):
                k = o * GROUP + u
                rows = pl.ds(pl.multiple_of(k * extent, extent), extent)
                part = jnp.dot(source[rows, :], weights[...], preferred_element_type=jnp.float32)
                if keep:
                    contracted[k] = part
                acc = acc + part * third_d[pl.ds(k, 1), :]
            return acc

        acc = lax.fori_loop(0, K // GROUP, step, jnp.zeros((extent, 2 * R), jnp.float32))
        return acc + swap_halves(acc)

    BLOCKS = R // PANEL

    def sweep(_, carry):
        weights[...] = split_weights(second_d[...])
        m1_buf[my_col] = pack(contract(by_row, I, False))
        m1_copies = start(col_copies(0, m1_buf))
        system, by_lane, _ = balance(gram3[...] * gram2[...])
        inv = sweep_blocks(system, BLOCKS)
        around = by_lane * scale2_row[...]
        wait(m1_copies)
        raw1 = solve_packed(total(m1_buf, nc) * around, inv) * (around * third_inv[...])

        packed = pack(gram_doubled(raw1, R))
        share = packed.shape[0] // nc
        for c in range(nc):
            g1_src[c] = packed[c * share : (c + 1) * share]
        g1_buf[my_row] = g1_src[my_col]
        g1_copies = start(row_copies(0, g1_buf, g1_buf))
        weights[...] = split_weights(raw1)
        packed = pack(contract(by_col, J, True))
        share = packed.shape[0] // nr
        for r in range(nr):
            m2_src[r] = packed[r * share : (r + 1) * share]
        m2_buf[my_row] = m2_src[my_row]
        m2_copies = start(row_copies(1, m2_src, m2_buf, scatter=True))
        wait(g1_copies)
        g1_all[my_col] = total(g1_buf, nr)
        g1_copies = start(col_copies(2, g1_all))
        wait(m2_copies)
        m2_all[my_row] = total(m2_buf, nr)
        m2_copies = start(row_copies(2, m2_all, m2_all))
        wait(g1_copies)

        gram1 = unpack(joined(g1_all, nc))
        system, by_lane1, by_sub1 = balance(gram3[...] * gram1)
        inv = sweep_blocks(system, BLOCKS)
        gram1 = gram1 * by_sub1 * by_lane1
        scale1 = col_scale(unpack(joined(g1_all, nc)), I * nr)
        inv_scale1 = 1.0 / scale1
        first_d[...] = raw1 * inv_scale1
        wait(m2_copies)
        raw2 = solve_packed(joined(m2_all, nr) * by_lane1, inv) * (by_lane1 * scale1)
        g2_buf[my_col] = pack(gram_doubled(raw2, R))
        g2_copies = start(col_copies(1, g2_buf))

        scaled = raw2 * inv_scale1
        for k in range(K):
            m3_rows[k : k + 1] = jnp.sum(contracted[k] * scaled, axis=0, keepdims=True)
        m3 = m3_rows[...]
        m3_buf[my_row] = pack(m3 + swap_halves(m3))
        m3_copies = start(row_copies(3, m3_buf, m3_buf))
        wait(g2_copies)
        gram = unpack(total(g2_buf, nc))
        gram2[...] = gram
        system, by_lane, _ = balance(gram1 * gram)
        inv = sweep_blocks(system, BLOCKS // 2)
        wait(m3_copies)
        m3_all[my_col] = total(m3_buf, nr)
        m3_copies = start(col_copies(3, m3_all))
        inv = sweep_blocks(inv, BLOCKS - BLOCKS // 2)
        scale2 = col_scale(gram, J * nc)
        scale2_row[...] = scale2
        second_d[...] = raw2 * (1.0 / scale2)
        around = by_lane * by_lane1 * scale1
        wait(m3_copies)
        third = solve_packed(total(m3_all, nc) * around, inv) * (around * scale2)
        third_raw[...] = third
        settle_third(third)
        return carry

    lax.fori_loop(0, ITERS, sweep, 0)
    first_out[...] = first_d[:, :R]
    second_out[...] = second_d[:, :R]
    third_out[...] = third_raw[:, :R]


def per_device(nr, nc, tensor, second_init, third_init):
    K, I, J = tensor.shape
    R = second_init.shape[1]
    wide = 2 * R
    f32 = jnp.float32
    half = R // 2

    def vmem(*shape):
        return pltpu.VMEM(shape, f32)

    return pl.pallas_call(
        functools.partial(kernel, nr, nc),
        out_shape=(
            jax.ShapeDtypeStruct((I, R), f32),
            jax.ShapeDtypeStruct((J, R), f32),
            jax.ShapeDtypeStruct((K, R), f32),
        ),
        in_specs=[pl.BlockSpec(memory_space=pltpu.VMEM)] * 3,
        out_specs=(pl.BlockSpec(memory_space=pltpu.VMEM),) * 3,
        scratch_shapes=[
            pltpu.VMEM((K * I, 2 * J), jnp.bfloat16),
            pltpu.VMEM((K * J, 2 * I), jnp.bfloat16),
            vmem(K, J, wide),
            pltpu.VMEM((2 * J, wide), jnp.bfloat16),
            vmem(I, wide),
            vmem(J, wide),
            vmem(K, wide),
            vmem(K, wide),
            vmem(1, wide),
            vmem(1, wide),
            vmem(R, wide),
            vmem(R, wide),
            vmem(K, wide),
            vmem(nc, I // 2, wide),
            vmem(nc, half // nc, wide),
            vmem(nr, half // nc, wide),
            vmem(nc, half // nc, wide),
            vmem(nr, J // 2 // nr, wide),
            vmem(nr, J // 2 // nr, wide),
            vmem(nr, J // 2 // nr, wide),
            vmem(nc, half, wide),
            vmem(nr, K // 2, wide),
            vmem(nc, K // 2, wide),
            pltpu.SemaphoreType.DMA((4, nc - 1)),
            pltpu.SemaphoreType.DMA((4, nc - 1)),
            pltpu.SemaphoreType.DMA((4, nr - 1)),
            pltpu.SemaphoreType.DMA((4, nr - 1)),
        ],
        compiler_params=pltpu.CompilerParams(
            collective_id=0, has_side_effects=True, vmem_limit_bytes=32 * 1024 * 1024
        ),
        cost_estimate=pl.CostEstimate(
            flops=ITERS * 2 * 2 * K * I * J * 2 * wide, bytes_accessed=4 * K * I * J, transcendentals=0
        ),
        name="als_sweeps",
    )(tensor, second_init.T, third_init)


def solution(mesh):
    return jax.shard_map(
        functools.partial(per_device, mesh.shape["rows"], mesh.shape["cols"]),
        mesh=mesh,
        in_specs=(P(None, "rows", "cols"), P("cols", None), P()),
        out_specs=(P("rows", None), P("cols", None), P()),
        check_vma=False,
    )
```

```python
import functools

import jax
import jax.numpy as jnp
from jax import lax
from jax.experimental import pallas as pl
from jax.experimental.pallas import tpu as pltpu
from jax.sharding import PartitionSpec as P

ITERS = 5
EPSILON = 1e-05
MESH = pl.DeviceIdType.MESH
PANEL = 8


def lane_of(shape):
    return lax.broadcasted_iota(jnp.int32, shape, len(shape) - 1)


def swap_halves(x):
    return pltpu.roll(x, x.shape[1] // 2, axis=1)


def pack(x):
    n = x.shape[0] // 2
    return jnp.where(lane_of((n, x.shape[1])) < x.shape[1] // 2, x[:n], x[n:])


def unpack(x):
    other = swap_halves(x)
    left = lane_of(x.shape) < x.shape[1] // 2
    return jnp.concatenate([jnp.where(left, x, other), jnp.where(left, other, x)], axis=0)


def split_halves(x):
    high = x.astype(jnp.bfloat16).astype(jnp.float32)
    return jnp.where(lane_of(x.shape) < x.shape[1] // 2, high, x - high).astype(jnp.bfloat16)


def gram_doubled(x, rank):
    left = split_halves(x)
    high = x.T.astype(jnp.bfloat16).astype(jnp.float32)
    parts = x.T - high
    rows = lax.broadcasted_iota(jnp.int32, parts.shape, 0)
    turned = jnp.where(rows < rank, high, parts).astype(jnp.bfloat16)
    all_four = jnp.dot(turned, left, preferred_element_type=jnp.float32)
    both = all_four[:rank] + all_four[rank:]
    return both + swap_halves(both)


def diag_mask(rank, wide):
    rows = lax.broadcasted_iota(jnp.int32, (rank, wide), 0)
    lanes = lane_of((rank, wide))
    return (lanes == rows) | (lanes == rows + rank)


def col_scale(raw_gram, total):
    diag = jnp.where(diag_mask(*raw_gram.shape), raw_gram, 0.0)
    return jnp.sqrt(jnp.sum(diag, axis=0, keepdims=True) / total + EPSILON)


def balance(system):
    diag = jnp.where(diag_mask(*system.shape), system, 0.0)
    by_lane = lax.rsqrt(jnp.sum(diag, axis=0, keepdims=True))
    by_sub = lax.rsqrt(0.5 * jnp.sum(diag, axis=1, keepdims=True))
    return system * by_sub * by_lane, by_lane, by_sub


def sweep_blocks(a, count):
    rank, wide = a.shape
    tiles = rank // PANEL
    tile = (PANEL, wide)
    lane = lane_of(tile) % rank
    sub = lax.broadcasted_iota(jnp.int32, tile, 0)

    def row(x, p):
        return jnp.broadcast_to(x[p : p + 1], tile)

    def block(_, a):
        head, rest = a[:PANEL], a[PANEL:].reshape(tiles - 1, PANEL, wide)
        cols = [jnp.broadcast_to(head[:, q : q + 1], tile) for q in range(PANEL)]
        for p in range(0, PANEL, 2):
            u, v = cols[p], cols[p + 1]
            uu, uv, vv = row(u, p), row(u, p + 1), row(v, p + 1)
            inv = 1.0 / (uu * vv - uv * uv)
            iu, iv, ic = vv * inv, uu * inv, -(uv * inv)

            def reduced(x):
                x0, x1 = row(x, p), row(x, p + 1)
                return iu * x0 + ic * x1, ic * x0 + iv * x1

            def put(x, top, low):
                new = x - u * top - v * low
                return jnp.where(sub == p, top, jnp.where(sub == p + 1, low, new))

            for q in range(p + 2, PANEL):
                cols[q] = put(cols[q], *reduced(cols[q]))
            top, low = reduced(head)
            at_u, at_v = lane == p, lane == p + 1
            top = jnp.where(at_u, -iu, jnp.where(at_v, -ic, top))
            low = jnp.where(at_u, -ic, jnp.where(at_v, -iv, low))
            head = put(jnp.where(at_u | at_v, 0.0, head), top, low)
        new = jnp.where((lane < PANEL)[None], 0.0, rest)
        for q in range(PANEL):
            new = new - jnp.broadcast_to(rest[:, :, q : q + 1], rest.shape) * row(head, q)
        a = jnp.concatenate([new.reshape(rank - PANEL, wide), head], axis=0)
        return pltpu.roll(a, wide - PANEL, axis=1)

    return lax.fori_loop(0, count, block, a)


def solve_packed(packed, minus_inv):
    parts = split_halves(-minus_inv)
    weights = jnp.concatenate([parts, parts], axis=0)
    out = jnp.dot(split_halves(unpack(packed)), weights, preferred_element_type=jnp.float32)
    return out + swap_halves(out)


def split_weights(x):
    mixed = split_halves(x)
    return jnp.concatenate([mixed, mixed], axis=0)


def kernel(
    nr,
    nc,
    tensor,
    second_in,
    third_in,
    first_out,
    second_out,
    third_out,
    by_row,
    by_col,
    contracted,
    weights,
    first_d,
    second_d,
    third_d,
    third_raw,
    third_inv,
    scale2_row,
    gram2,
    gram3,
    m3_rows,
    m1_buf,
    g1_src,
    g1_buf,
    g1_all,
    m2_src,
    m2_buf,
    m2_all,
    g2_buf,
    m3_buf,
    m3_all,
    col_send,
    col_recv,
    row_send,
    row_recv,
):
    K, I, J = tensor.shape
    R = second_in.shape[0]
    my_row = lax.axis_index("rows")
    my_col = lax.axis_index("cols")

    def col_peer(d):
        return lax.rem(my_col + d, nc)

    def row_peer(d):
        return lax.rem(my_row + d, nr)

    def col_copies(kind, buf):
        return [
            pltpu.make_async_remote_copy(
                src_ref=buf.at[my_col],
                dst_ref=buf.at[my_col],
                send_sem=col_send.at[kind, d - 1],
                recv_sem=col_recv.at[kind, d - 1],
                device_id=(my_row, col_peer(d)),
                device_id_type=MESH,
            )
            for d in range(1, nc)
        ]

    def row_copies(kind, src, dst, scatter=False):
        return [
            pltpu.make_async_remote_copy(
                src_ref=src.at[row_peer(d)] if scatter else src.at[my_row],
                dst_ref=dst.at[my_row],
                send_sem=row_send.at[kind, d - 1],
                recv_sem=row_recv.at[kind, d - 1],
                device_id=(row_peer(d), my_col),
                device_id_type=MESH,
            )
            for d in range(1, nr)
        ]

    def start(copies):
        for copy in copies:
            copy.start()
        return copies

    def wait(copies):
        for copy in copies:
            copy.wait()

    def total(buf, n):
        out = buf[0]
        for s in range(1, n):
            out = out + buf[s]
        return out

    def joined(buf, n):
        return jnp.concatenate([buf[s] for s in range(n)], axis=0)

    barrier = pltpu.get_barrier_semaphore()
    for d in range(1, nc):
        pl.semaphore_signal(barrier, inc=1, device_id=(my_row, col_peer(d)), device_id_type=MESH)
    for d in range(1, nr):
        pl.semaphore_signal(barrier, inc=1, device_id=(row_peer(d), my_col), device_id_type=MESH)

    GROUP = 8
    start_second = second_in[...]
    start_second = jnp.concatenate([start_second, start_second], axis=0).T
    start_third = third_in[...]
    start_third = jnp.concatenate([start_third, start_third], axis=1)
    g2_buf[my_col] = pack(gram_doubled(start_second, R))
    pl.semaphore_wait(barrier, nc - 1 + nr - 1)
    copies = start(col_copies(1, g2_buf))

    def settle_third(third):
        inv_norm = 1.0 / jnp.sqrt(jnp.sum(third * third, axis=0, keepdims=True))
        unit = third * inv_norm
        third_d[...] = unit
        third_inv[...] = inv_norm
        gram3[...] = gram_doubled(unit, R)

    settle_third(start_third)

    def split_slice(k, _):
        rows = pl.ds(pl.multiple_of(k * I, I), I)
        block = tensor[k]
        high = block.astype(jnp.bfloat16)
        by_row[rows, :J] = high
        by_row[rows, J:] = (block - high.astype(jnp.float32)).astype(jnp.bfloat16)
        turned = block.T
        rows = pl.ds(pl.multiple_of(k * J, J), J)
        high = turned.astype(jnp.bfloat16)
        by_col[rows, :I] = high
        by_col[rows, I:] = (turned - high.astype(jnp.float32)).astype(jnp.bfloat16)
        return 0

    lax.fori_loop(0, K, split_slice, 0)
    wait(copies)
    gram = unpack(total(g2_buf, nc))
    gram2[...] = gram
    scale = col_scale(gram, J * nc)
    scale2_row[...] = scale
    second_d[...] = start_second / scale

    def contract(source, extent, keep):
        def step(o, acc):
            for u in range(GROUP):
                k = o * GROUP + u
                rows = pl.ds(pl.multiple_of(k * extent, extent), extent)
                part = jnp.dot(source[rows, :], weights[...], preferred_element_type=jnp.float32)
                if keep:
                    contracted[k] = part
                acc = acc + part * third_d[pl.ds(k, 1), :]
            return acc

        acc = lax.fori_loop(0, K // GROUP, step, jnp.zeros((extent, 2 * R), jnp.float32))
        return acc + swap_halves(acc)

    BLOCKS = R // PANEL

    def sweep(_, carry):
        weights[...] = split_weights(second_d[...])
        m1_buf[my_col] = pack(contract(by_row, I, False))
        m1_copies = start(col_copies(0, m1_buf))
        system, by_lane, _ = balance(gram3[...] * gram2[...])
        inv = sweep_blocks(system, BLOCKS)
        around = by_lane * scale2_row[...]
        wait(m1_copies)
        raw1 = solve_packed(total(m1_buf, nc) * around, inv) * (around * third_inv[...])

        packed = pack(gram_doubled(raw1, R))
        share = packed.shape[0] // nc
        for c in range(nc):
            g1_src[c] = packed[c * share : (c + 1) * share]
        g1_buf[my_row] = g1_src[my_col]
        g1_copies = start(row_copies(0, g1_buf, g1_buf))
        weights[...] = split_weights(raw1)
        packed = pack(contract(by_col, J, True))
        share = packed.shape[0] // nr
        for r in range(nr):
            m2_src[r] = packed[r * share : (r + 1) * share]
        m2_buf[my_row] = m2_src[my_row]
        m2_copies = start(row_copies(1, m2_src, m2_buf, scatter=True))
        wait(g1_copies)
        g1_all[my_col] = total(g1_buf, nr)
        g1_copies = start(col_copies(2, g1_all))
        wait(m2_copies)
        m2_all[my_row] = total(m2_buf, nr)
        m2_copies = start(row_copies(2, m2_all, m2_all))
        wait(g1_copies)

        gram1 = unpack(joined(g1_all, nc))
        system, by_lane1, by_sub1 = balance(gram3[...] * gram1)
        inv = sweep_blocks(system, BLOCKS)
        gram1 = gram1 * by_sub1 * by_lane1
        scale1 = col_scale(unpack(joined(g1_all, nc)), I * nr)
        inv_scale1 = 1.0 / scale1
        first_d[...] = raw1 * inv_scale1
        wait(m2_copies)
        raw2 = solve_packed(joined(m2_all, nr) * by_lane1, inv) * (by_lane1 * scale1)
        g2_buf[my_col] = pack(gram_doubled(raw2, R))
        g2_copies = start(col_copies(1, g2_buf))

        scaled = raw2 * inv_scale1
        for k in range(K):
            m3_rows[k : k + 1] = jnp.sum(contracted[k] * scaled, axis=0, keepdims=True)
        m3 = m3_rows[...]
        m3_buf[my_row] = pack(m3 + swap_halves(m3))
        m3_copies = start(row_copies(3, m3_buf, m3_buf))
        wait(g2_copies)
        gram = unpack(total(g2_buf, nc))
        gram2[...] = gram
        system, by_lane, _ = balance(gram1 * gram)
        wait(m3_copies)
        m3_all[my_col] = total(m3_buf, nr)
        m3_copies = start(col_copies(3, m3_all))
        inv = sweep_blocks(system, BLOCKS)
        scale2 = col_scale(gram, J * nc)
        scale2_row[...] = scale2
        second_d[...] = raw2 * (1.0 / scale2)
        around = by_lane * by_lane1 * scale1
        wait(m3_copies)
        third = solve_packed(total(m3_all, nc) * around, inv) * (around * scale2)
        third_raw[...] = third
        settle_third(third)
        return carry

    lax.fori_loop(0, ITERS, sweep, 0)
    first_out[...] = first_d[:, :R]
    second_out[...] = second_d[:, :R]
    third_out[...] = third_raw[:, :R]


def per_device(nr, nc, tensor, second_init, third_init):
    K, I, J = tensor.shape
    R = second_init.shape[1]
    wide = 2 * R
    f32 = jnp.float32
    half = R // 2

    def vmem(*shape):
        return pltpu.VMEM(shape, f32)

    return pl.pallas_call(
        functools.partial(kernel, nr, nc),
        out_shape=(
            jax.ShapeDtypeStruct((I, R), f32),
            jax.ShapeDtypeStruct((J, R), f32),
            jax.ShapeDtypeStruct((K, R), f32),
        ),
        in_specs=[pl.BlockSpec(memory_space=pltpu.VMEM)] * 3,
        out_specs=(pl.BlockSpec(memory_space=pltpu.VMEM),) * 3,
        scratch_shapes=[
            pltpu.VMEM((K * I, 2 * J), jnp.bfloat16),
            pltpu.VMEM((K * J, 2 * I), jnp.bfloat16),
            vmem(K, J, wide),
            pltpu.VMEM((2 * J, wide), jnp.bfloat16),
            vmem(I, wide),
            vmem(J, wide),
            vmem(K, wide),
            vmem(K, wide),
            vmem(1, wide),
            vmem(1, wide),
            vmem(R, wide),
            vmem(R, wide),
            vmem(K, wide),
            vmem(nc, I // 2, wide),
            vmem(nc, half // nc, wide),
            vmem(nr, half // nc, wide),
            vmem(nc, half // nc, wide),
            vmem(nr, J // 2 // nr, wide),
            vmem(nr, J // 2 // nr, wide),
            vmem(nr, J // 2 // nr, wide),
            vmem(nc, half, wide),
            vmem(nr, K // 2, wide),
            vmem(nc, K // 2, wide),
            pltpu.SemaphoreType.DMA((4, nc - 1)),
            pltpu.SemaphoreType.DMA((4, nc - 1)),
            pltpu.SemaphoreType.DMA((4, nr - 1)),
            pltpu.SemaphoreType.DMA((4, nr - 1)),
        ],
        compiler_params=pltpu.CompilerParams(
            collective_id=0, has_side_effects=True, vmem_limit_bytes=32 * 1024 * 1024
        ),
        cost_estimate=pl.CostEstimate(
            flops=ITERS * 2 * 2 * K * I * J * 2 * wide, bytes_accessed=4 * K * I * J, transcendentals=0
        ),
        name="als_sweeps",
    )(tensor, second_init.T, third_init)


def solution(mesh):
    return jax.shard_map(
        functools.partial(per_device, mesh.shape["rows"], mesh.shape["cols"]),
        mesh=mesh,
        in_specs=(P(None, "rows", "cols"), P("cols", None), P()),
        out_specs=(P("rows", None), P("cols", None), P()),
        check_vma=False,
    )
```
